512 devices in a mesh: ang: 32 (over z, x_lo, core), xy: 16 (over y, x_hi).
Axes of the slice: x: 4 (x_hi: 2, x_lo: 2; x = x_hi * 2 + x_lo), y: 8, z: 8, core: 2. Of those that a mesh axis runs over, the one named last changes fastest.
Arguments:
- contrast: float32 [32, 2, 1024, 2048], P('ang', None, 'xy'), may hold values from -4 to 4
- owners: int32 [3], replicated, may hold values from 0 to 31, as said below
- tilts: int32 [32, 2], P('ang'), may hold values from -8 to 8
Outputs:
- exit_real: float32 [32, 1024, 2048], P('ang', 'xy')
- exit_imag: float32 [32, 1024, 2048], P('ang', 'xy')
The draws below stay inside these ranges and needn't reach their ends.
Inputs may be any that keep to these rules, and one draw needn't show every extreme that they name: `owners`: the 3 entries are distinct.
All inputs are finite; a program needn't handle non-finite values.
Results may differ from the reference program's by a relative error of at most 0.0003.
Values sent between devices are 32-bit elements; how exact they have to be, the bound alone decides.
No kernel may reach another device: no remote copies, remote signals or barrier semaphores. Data moves between devices by JAX's collectives and lax.ppermute only.
A program may use at most 64 MiB of HBM per device.

```python
import math
import jax
import jax.numpy as jnp
from jax import lax

COLS = 2048
DZ = 2
SLABS = 3
ILLUM = 32
NX = 1024
N_ANG = 32


def draw_owners(key, part):
    key = jax.random.fold_in(key, 11)
    order = jax.random.permutation(key, N_ANG)[:SLABS].astype(jnp.int32)
    highest = jnp.max(order)
    lowest = jnp.min(order)
    order = jnp.where(order == highest, N_ANG - 1, order)
    order = jnp.where(order == lowest, 0, order)
    return order.astype(jnp.int32)


def plant(array, own_key, least, top_value):
    shape = array.shape
    index_at = [jax.random.randint(jax.random.fold_in(own_key, axis), (), 0, shape[axis]) for axis in range(len(shape))]
    array = array.at[tuple(index_at)].set(least)
    longest = shape.index(max(shape))
    index_at[longest] = (index_at[longest] + 1) % shape[longest]
    return array.at[tuple(index_at)].set(top_value)


def level_of(own_key, extent, pieces, low, largest):
    factor_of = 1.0
    for position, parts in pieces:
        steps = jax.random.uniform(jax.random.fold_in(jax.random.fold_in(own_key, 6), position), (parts,), jnp.float32, low / len(pieces), largest / len(pieces))
        factor_of = factor_of * jnp.repeat(jnp.exp(steps), extent[position] // parts).reshape((-1,) + (1,) * (len(extent) - 1 - position))
    return factor_of


def normal_values(key, shape, scale, bound, shards=(), kind=jnp.bfloat16):
    result = scale * jax.random.normal(key, shape, jnp.float32)
    if shards:
        result = result * level_of(key, shape, shards, -0.22, 0.18)
    return jnp.clip(result, -bound, bound).astype(kind)


def setup_inputs(seed: int = 0) -> dict:
    key_list = jax.random.split(jax.random.key(seed), 4)
    contrast = normal_values(key_list[0], (N_ANG, DZ, NX, COLS), 1.0, 4.0, ((0, 32), (2, 16)), jnp.float32)
    owners = draw_owners(jax.random.fold_in(key_list[3], 71), 0)
    tilts = plant(jax.random.randint(key_list[2], (ILLUM, 2), -8, 9), jax.random.fold_in(key_list[2], 1), -8, 8).astype(jnp.int32)
    return {"contrast": contrast, "owners": owners, "tilts": tilts}


diffraction = 0.05
phase_gain = 0.08


def incident(tilts, first, rows, total_rows, cols):
    row_ids = first + jnp.arange(rows, dtype=jnp.int32)
    col_ids = jnp.arange(cols, dtype=jnp.int32)
    along_rows = (tilts[:, 0:1] * row_ids[None, :]) % total_rows
    along_cols = (tilts[:, 1:2] * col_ids[None, :]) % cols
    angle = (2.0 * math.pi) * (along_rows.astype(jnp.float32) / total_rows)[:, :, None]
    angle = angle + (2.0 * math.pi) * (along_cols.astype(jnp.float32) / cols)[:, None, :]
    return jnp.stack([jnp.cos(angle), jnp.sin(angle)])


def laplace(values):
    middle = values[..., 1:-1, :]
    widths = [(0, 0)] * (middle.ndim - 1) + [(1, 1)]
    sides = jnp.pad(middle, widths)
    return values[..., :-2, :] + values[..., 2:, :] + sides[..., :-2] + sides[..., 2:] - 4.0 * middle


def slope(values, plane):
    inner = diffraction * laplace(values) + phase_gain * plane * values[..., 1:-1, :]
    return jnp.stack([-inner[1], inner[0]])


def heun(field, plane_outer, plane_inner, valid_outer, valid_inner):
    first = slope(field, plane_outer)
    trial = (field[..., 1:-1, :] + first) * valid_outer
    second = slope(trial, plane_inner)
    return (field[..., 2:-2, :] + 0.5 * (first[..., 1:-1, :] + second)) * valid_inner


def reference(contrast, owners, tilts):
    field = incident(tilts, 0, NX, NX, COLS)
    valid_outer = jnp.pad(jnp.ones((NX, 1), jnp.float32), ((1, 1), (0, 0)))
    valid_inner = jnp.ones((NX, 1), jnp.float32)
    for slab_id in range(SLABS):
        slab = lax.dynamic_index_in_dim(contrast, owners[slab_id], 0, keepdims=False)

        def advance(j, state):
            plane = lax.dynamic_index_in_dim(slab, j, 0, keepdims=False)
            padded = jnp.pad(state, ((0, 0), (0, 0), (2, 2), (0, 0)))
            outer = jnp.pad(plane, ((1, 1), (0, 0)))
            return heun(padded, outer, plane, valid_outer, valid_inner)

        field = lax.fori_loop(0, DZ, advance, field)
    return field[0], field[1]
```

```python
import functools
import math

import jax
import jax.numpy as jnp
from jax import lax
from jax.experimental import pallas as pl
from jax.experimental.pallas import tpu as pltpu
from jax.sharding import PartitionSpec as P

diffraction = 0.05
phase_gain = 0.08

HALO = (12, 8, 4)
TOP = 24
ROWS = 112
LANES = 128

TRIAL = ((1, 13), (1, 13), (2, 12), (2, 12), (2, 12), (2, 12))
FIELD = ((1, 13), (2, 12), (2, 12), (2, 12), (2, 12), (3, 11))


def neighbours(tile, above, below, cols, row, lane):
    sums = []
    for c in range(cols):
        here = tile[c]
        zero = jnp.zeros_like(here)
        west = tile[c - 1] if c else zero
        east = tile[c + 1] if c < cols - 1 else zero
        up = pltpu.roll(jnp.where(row == 7, above[c], here), 1, 0)
        down = pltpu.roll(jnp.where(row == 0, below[c], here), 7, 0)
        left = pltpu.roll(jnp.where(lane == LANES - 1, west, here), 1, 1)
        right = pltpu.roll(jnp.where(lane == 0, east, here), LANES - 1, 1)
        sums.append((up + down) + (left + right))
    return sums


def load(ref, part, i, cols):
    at = pl.ds(pl.multiple_of(i * 8, 8), 8)
    return [ref[part, at, c * LANES : (c + 1) * LANES] for c in range(cols)]


def coupled(ref, part, i, plane, cols, row, lane):
    here = load(ref, part, i, cols)
    around = neighbours(here, load(ref, part, i - 1, cols), load(ref, part, i + 1, cols), cols, row, lane)
    return here, [s + p * h for s, p, h in zip(around, plane, here)]


def assemble(place, refs, planes, slab, skip, cols):
    count, to = 64 + 2 * HALO[slab], TOP - HALO[slab]
    for ref, core, half in refs:
        plane = place[1] if core == 0 else 1 - place[1]
        column = place[0] if half == 0 else 1 - place[0]
        for z in range(cols // 2):
            at = pl.ds(pl.multiple_of((2 * z + column) * LANES, LANES), LANES)
            values = ref[z, skip : skip + count, :]
            planes[plane, to : to + count, at] = (phase_gain / diffraction) * values - 4.0


def clear(refs):
    for ref in refs:
        blank = jnp.zeros((TOP,) + ref.shape[2:], jnp.float32)
        for part in range(2):
            ref[part, 0:TOP, :] = blank
            ref[part, TOP + 64 : ROWS, :] = blank


def advance(place, s, plane_ref, field, trial, after, cols):
    row = lax.broadcasted_iota(jnp.int32, (8, LANES), 0)
    lane = lax.broadcasted_iota(jnp.int32, (8, LANES), 1)
    low, high = bounds(place)

    def first(i, carry):
        at = pl.ds(pl.multiple_of(i * 8, 8), 8)
        plane = [plane_ref[at, c * LANES : (c + 1) * LANES] for c in range(cols)]
        re, a = coupled(field, 0, i, plane, cols, row, lane)
        for c in range(cols):
            span = slice(c * LANES, (c + 1) * LANES)
            trial[1, at, span] = field[1, at, span] + diffraction * a[c]
        im, b = coupled(field, 1, i, plane, cols, row, lane)
        for c in range(cols):
            span = slice(c * LANES, (c + 1) * LANES)
            trial[0, at, span] = re[c] - diffraction * b[c]
        return carry

    def second(i, carry):
        at = pl.ds(pl.multiple_of(i * 8, 8), 8)
        to = pl.ds(pl.multiple_of((i - after[1]) * 8, 8), 8)
        plane = [plane_ref[at, c * LANES : (c + 1) * LANES] for c in range(cols)]
        re, a = coupled(trial, 0, i, plane, cols, row, lane)
        for c in range(cols):
            span = slice(c * LANES, (c + 1) * LANES)
            old = field[1, at, span] + trial[1, at, span]
            after[0][1][to, span] = 0.5 * old + (0.5 * diffraction) * a[c]
        im, b = coupled(trial, 1, i, plane, cols, row, lane)
        for c in range(cols):
            span = slice(c * LANES, (c + 1) * LANES)
            old = field[0, at, span] + re[c]
            after[0][0][to, span] = 0.5 * old - (0.5 * diffraction) * b[c]
        return carry

    lax.fori_loop(jnp.maximum(low, TRIAL[s][0]), jnp.minimum(high, TRIAL[s][1]), first, 0)
    lax.fori_loop(jnp.maximum(low, FIELD[s][0]), jnp.minimum(high, FIELD[s][1]), second, 0)


def bounds(place):
    low = jnp.where(place[2] == 0, TOP // 8, 0)
    high = jnp.where(place[2] == place[3], TOP // 8 + 8, ROWS // 8)
    return low, high


def incident(rowwave, colwave, field, place, cols):
    low, high = bounds(place)

    def start(i, carry):
        at = pl.ds(pl.multiple_of(i * 8, 8), 8)
        c_row, s_row = rowwave[0, at, :], rowwave[1, at, :]
        for c in range(cols):
            span = slice(c * LANES, (c + 1) * LANES)
            c_col, s_col = colwave[0, :, span], colwave[1, :, span]
            field[0, at, span] = c_row * c_col - s_row * s_col
            field[1, at, span] = s_row * c_col + c_row * s_col
        return carry

    lax.fori_loop(jnp.maximum(low, 1), jnp.minimum(high, ROWS // 8 - 1), start, 0)


def through(*refs, slab, skip, cols, first, last):
    refs = list(refs)
    place = refs.pop(0)
    waves = [refs.pop(0) for _ in range(2)] if first else []
    before = None if first else refs.pop(0)
    mine, other, theirs = refs[:3]
    planes, trial, field = refs[-3:]
    pieces = ((mine, 0, 0), (other, 0, 1), (theirs.at[0], 1, 0), (theirs.at[1], 1, 1))
    assemble(place, pieces, planes, slab, skip, cols)
    clear((trial, field))
    if first:
        incident(*waves, field, place, cols)
        before = field
    middle = (field.at[0], field.at[1]), 0
    if last:
        after = (refs[3].at[0], refs[4].at[0]), TOP // 8
    else:
        clear((refs[3],))
        after = (refs[3].at[0], refs[3].at[1]), 0
    advance(place, 2 * slab, planes.at[0], before, trial, middle, cols)
    advance(place, 2 * slab + 1, planes.at[1], field, trial, after, cols)


def waves(tilts, anchor, total_rows, cols):
    row_ids = anchor - TOP + jnp.arange(ROWS, dtype=jnp.int32)
    col_ids = jnp.arange(cols, dtype=jnp.int32)
    along_rows = (tilts[0, 0] * row_ids) % total_rows
    along_cols = (tilts[0, 1] * col_ids) % cols
    row_angle = 2.0 * math.pi * (along_rows.astype(jnp.float32) / total_rows)
    col_angle = 2.0 * math.pi * (along_cols.astype(jnp.float32) / cols)
    by_row = jnp.stack([jnp.cos(row_angle), jnp.sin(row_angle)])
    by_col = jnp.stack([jnp.cos(col_angle), jnp.sin(col_angle)])
    return (
        jnp.broadcast_to(by_row[:, :, None], (2, ROWS, LANES)),
        jnp.broadcast_to(by_col[:, None, :], (2, 8, cols)),
    )


def keep(contrast, owners):
    rows, cols = contrast.shape[1:]
    angs = lax.axis_size("ang")
    chips = angs // 2
    chip = lax.axis_index("ang") // 2
    by_chip = [[2 * i + c for i in range(chips)] for c in range(2)]
    by_core = [[2 * i, 2 * i + 1] for i in range(chips)]
    planes = lax.all_to_all(contrast, "ang", 0, 0, tiled=True, axis_index_groups=by_core)
    owner_chip, owner_core = owners // 2, owners % 2

    def one():
        core = jnp.sum(jnp.where(owner_chip == chip, owner_core, 0))
        plane = lax.dynamic_index_in_dim(planes, core, 0, keepdims=False)
        tiles = plane.reshape(rows, chips, cols // chips).transpose(1, 0, 2)
        tiles = lax.all_to_all(tiles, "ang", 0, 0, tiled=True, axis_index_groups=by_chip)
        return tuple(lax.dynamic_index_in_dim(tiles, c, 0, keepdims=False) for c in owner_chip)

    def both():
        tiles = planes.reshape(2, rows, chips, cols // chips).transpose(2, 0, 1, 3)
        tiles = lax.all_to_all(tiles, "ang", 0, 0, tiled=True, axis_index_groups=by_chip)
        tiles = tiles.reshape(angs, rows, cols // chips)
        return tuple(lax.dynamic_index_in_dim(tiles, o, 0, keepdims=False) for o in owners)

    shared = (owner_chip[:, None] == owner_chip[None, :]).sum() > owners.shape[0]
    return lax.cond(shared, both, one)


def per_device(contrast, owners, tilts):
    depth, rows, cols = contrast.shape[1:]
    slabs = owners.shape[0]
    spots = lax.axis_size("xy")
    ang = lax.axis_index("ang")
    spot = lax.axis_index("xy")
    angs = lax.axis_size("ang")

    kept = keep(contrast[0], owners)

    tails = jnp.concatenate([kept[k][rows - HALO[k] :] for k in range(slabs)], axis=0)
    heads = jnp.concatenate([kept[k][: HALO[k]] for k in range(slabs)], axis=0)
    above = lax.ppermute(tails, "xy", [(i, i + 1) for i in range(spots - 1)])
    below = lax.ppermute(heads, "xy", [(i + 1, i) for i in range(spots - 1)])

    columns = [[4 * z + q for z in range(angs // 4)] for q in range(4)]
    swap_x = [(i, i ^ 2) for i in range(angs)]
    swap_core = [(i, i ^ 1) for i in range(angs)]

    def along_z(chosen, after=None):
        parts = []
        for k in chosen:
            at = slice(sum(HALO[:k]), sum(HALO[: k + 1]))
            parts += [above[at], kept[k], below[at]]
        piece = jnp.concatenate(parts, axis=0)
        if after is not None:
            piece, after = lax.optimization_barrier((piece, after))
        copies = jnp.broadcast_to(piece, (angs // 4,) + piece.shape)
        return lax.all_to_all(copies, "ang", 0, 0, tiled=True, axis_index_groups=columns)

    def from_core(mine, other):
        return lax.ppermute(jnp.stack([mine, other]), "ang", swap_core)

    early, late = (0, 1), (2,)
    mine = along_z(early)
    other = lax.ppermute(mine, "ang", swap_x)
    late_mine = along_z(late, mine)
    late_mine, other = lax.optimization_barrier((late_mine, other))
    late_other = lax.ppermute(late_mine, "ang", swap_x)
    first = mine, other, from_core(mine, other)

    by_row, by_col = waves(tilts, spot * rows, rows * spots, cols)
    place = jnp.stack([ang // 2 % 2, ang % 2, spot, jnp.int32(spots - 1)])

    def step(slab, before, pieces):
        start, end = slab == 0, slab == slabs - 1
        state = jax.ShapeDtypeStruct((2, ROWS, cols), jnp.float32)
        out = jax.ShapeDtypeStruct((1, rows, cols), jnp.float32)
        in_vmem = pl.BlockSpec(memory_space=pltpu.VMEM)
        return pl.pallas_call(
            functools.partial(
                through,
                slab=slab,
                skip=sum(rows + 2 * HALO[k] for k in early if k < slab) if slab in early else 0,
                cols=cols // LANES,
                first=start,
                last=end,
            ),
            out_shape=(out, out) if end else state,
            in_specs=[pl.BlockSpec(memory_space=pltpu.SMEM)] + [in_vmem] * (len(before) + len(pieces)),
            out_specs=(in_vmem, in_vmem) if end else in_vmem,
            scratch_shapes=[
                pltpu.VMEM((depth, ROWS, cols), jnp.float32),
                pltpu.VMEM(state.shape, jnp.float32),
                pltpu.VMEM(state.shape, jnp.float32),
            ],
            compiler_params=pltpu.CompilerParams(vmem_limit_bytes=32 * 1024 * 1024),
            cost_estimate=pl.CostEstimate(flops=20_000_000, bytes_accessed=6_000_000, transcendentals=0),
        )(place, *before, *pieces)

    field = step(0, (by_row, by_col), first)
    late_other, field = lax.optimization_barrier((late_other, field))
    last = late_mine, late_other, from_core(late_mine, late_other)
    field = step(1, (field,), first)
    return step(2, (field,), last)


def solution(mesh):
    placed = (P("ang", None, "xy", None), P(), P("ang", None))
    return jax.shard_map(
        per_device,
        mesh=mesh,
        in_specs=placed,
        out_specs=(P("ang", "xy", None), P("ang", "xy", None)),
        check_vma=False,
    )
```

```python
import functools
import math

import jax
import jax.numpy as jnp
from jax import lax
from jax.experimental import pallas as pl
from jax.experimental.pallas import tpu as pltpu
from jax.sharding import PartitionSpec as P

diffraction = 0.05
phase_gain = 0.08

HALO = (12, 8, 4)
TOP = 24
ROWS = 112
LANES = 128

TRIAL = ((1, 13), (1, 13), (2, 12), (2, 12), (2, 12), (2, 12))
FIELD = ((1, 13), (2, 12), (2, 12), (2, 12), (2, 12), (3, 11))


def neighbours(tile, above, below, cols, row, lane):
    sums = []
    for c in range(cols):
        here = tile[c]
        zero = jnp.zeros_like(here)
        west = tile[c - 1] if c else zero
        east = tile[c + 1] if c < cols - 1 else zero
        up = pltpu.roll(jnp.where(row == 7, above[c], here), 1, 0)
        down = pltpu.roll(jnp.where(row == 0, below[c], here), 7, 0)
        left = pltpu.roll(jnp.where(lane == LANES - 1, west, here), 1, 1)
        right = pltpu.roll(jnp.where(lane == 0, east, here), LANES - 1, 1)
        sums.append((up + down) + (left + right))
    return sums


def load(ref, part, i, cols):
    at = pl.ds(pl.multiple_of(i * 8, 8), 8)
    return [ref[part, at, c * LANES : (c + 1) * LANES] for c in range(cols)]


def coupled(ref, part, i, plane, cols, row, lane):
    here = load(ref, part, i, cols)
    around = neighbours(here, load(ref, part, i - 1, cols), load(ref, part, i + 1, cols), cols, row, lane)
    return here, [s + p * h for s, p, h in zip(around, plane, here)]


def assemble(place, refs, planes, slab, skip, cols):
    count, to = 64 + 2 * HALO[slab], TOP - HALO[slab]
    for ref, core, half in refs:
        plane = place[1] if core == 0 else 1 - place[1]
        column = place[0] if half == 0 else 1 - place[0]
        for z in range(cols // 2):
            at = pl.ds(pl.multiple_of((2 * z + column) * LANES, LANES), LANES)
            values = ref[z, skip : skip + count, :]
            planes[plane, to : to + count, at] = (phase_gain / diffraction) * values - 4.0


def clear_outside(place, parts):
    @pl.when(place[2] == 0)
    def _():
        for ref in parts:
            ref[0:TOP, :] = jnp.zeros((TOP, ref.shape[1]), jnp.float32)

    @pl.when(place[2] == place[3])
    def _():
        for ref in parts:
            ref[TOP + 64 : ROWS, :] = jnp.zeros((ROWS - TOP - 64, ref.shape[1]), jnp.float32)


def advance(place, s, plane_ref, field, trial, after, cols):
    row = lax.broadcasted_iota(jnp.int32, (8, LANES), 0)
    lane = lax.broadcasted_iota(jnp.int32, (8, LANES), 1)

    def first(i, carry):
        at = pl.ds(pl.multiple_of(i * 8, 8), 8)
        plane = [plane_ref[at, c * LANES : (c + 1) * LANES] for c in range(cols)]
        re, a = coupled(field, 0, i, plane, cols, row, lane)
        for c in range(cols):
            span = slice(c * LANES, (c + 1) * LANES)
            trial[1, at, span] = field[1, at, span] + diffraction * a[c]
        im, b = coupled(field, 1, i, plane, cols, row, lane)
        for c in range(cols):
            span = slice(c * LANES, (c + 1) * LANES)
            trial[0, at, span] = re[c] - diffraction * b[c]
        return carry

    def second(i, carry):
        at = pl.ds(pl.multiple_of(i * 8, 8), 8)
        to = pl.ds(pl.multiple_of((i - after[1]) * 8, 8), 8)
        plane = [plane_ref[at, c * LANES : (c + 1) * LANES] for c in range(cols)]
        re, a = coupled(trial, 0, i, plane, cols, row, lane)
        for c in range(cols):
            span = slice(c * LANES, (c + 1) * LANES)
            old = field[1, at, span] + trial[1, at, span]
            after[0][1][to, span] = 0.5 * old + (0.5 * diffraction) * a[c]
        im, b = coupled(trial, 1, i, plane, cols, row, lane)
        for c in range(cols):
            span = slice(c * LANES, (c + 1) * LANES)
            old = field[0, at, span] + re[c]
            after[0][0][to, span] = 0.5 * old - (0.5 * diffraction) * b[c]
        return carry

    lax.fori_loop(*TRIAL[s], first, 0, unroll=True)
    clear_outside(place, (trial.at[0], trial.at[1]))
    lax.fori_loop(*FIELD[s], second, 0, unroll=True)


def incident(rowwave, colwave, field, cols):
    def start(i, carry):
        at = pl.ds(pl.multiple_of(i * 8, 8), 8)
        c_row, s_row = rowwave[0, at, :], rowwave[1, at, :]
        for c in range(cols):
            span = slice(c * LANES, (c + 1) * LANES)
            c_col, s_col = colwave[0, :, span], colwave[1, :, span]
            field[0, at, span] = c_row * c_col - s_row * s_col
            field[1, at, span] = s_row * c_col + c_row * s_col
        return carry

    lax.fori_loop(0, ROWS // 8, start, 0, unroll=2)


def through(*refs, slab, skip, cols, first, last):
    refs = list(refs)
    place = refs.pop(0)
    waves = [refs.pop(0) for _ in range(2)] if first else []
    before = None if first else refs.pop(0)
    mine, other, theirs = refs[:3]
    planes, trial, field = refs[-3:]
    pieces = ((mine, 0, 0), (other, 0, 1), (theirs.at[0], 1, 0), (theirs.at[1], 1, 1))
    assemble(place, pieces, planes, slab, skip, cols)
    if first:
        incident(*waves, field, cols)
        before = field
    middle = field.at[0], field.at[1]
    advance(place, 2 * slab, planes.at[0], before, trial, (middle, 0), cols)
    clear_outside(place, middle)
    if last:
        advance(place, 2 * slab + 1, planes.at[1], field, trial, ((refs[3].at[0], refs[4].at[0]), TOP // 8), cols)
    else:
        after = refs[3].at[0], refs[3].at[1]
        advance(place, 2 * slab + 1, planes.at[1], field, trial, (after, 0), cols)
        clear_outside(place, after)


def waves(tilts, anchor, total_rows, cols):
    row_ids = anchor - TOP + jnp.arange(ROWS, dtype=jnp.int32)
    col_ids = jnp.arange(cols, dtype=jnp.int32)
    along_rows = (tilts[0, 0] * row_ids) % total_rows
    along_cols = (tilts[0, 1] * col_ids) % cols
    row_angle = 2.0 * math.pi * (along_rows.astype(jnp.float32) / total_rows)
    col_angle = 2.0 * math.pi * (along_cols.astype(jnp.float32) / cols)
    inside = (row_ids >= 0) & (row_ids < total_rows)
    by_row = jnp.where(inside, jnp.stack([jnp.cos(row_angle), jnp.sin(row_angle)]), 0.0)
    by_col = jnp.stack([jnp.cos(col_angle), jnp.sin(col_angle)])
    return (
        jnp.broadcast_to(by_row[:, :, None], (2, ROWS, LANES)),
        jnp.broadcast_to(by_col[:, None, :], (2, 8, cols)),
    )


def keep(contrast, owners):
    rows, cols = contrast.shape[1:]
    angs = lax.axis_size("ang")
    chips = angs // 2
    chip = lax.axis_index("ang") // 2
    by_chip = [[2 * i + c for i in range(chips)] for c in range(2)]
    by_core = [[2 * i, 2 * i + 1] for i in range(chips)]
    planes = lax.all_to_all(contrast, "ang", 0, 0, tiled=True, axis_index_groups=by_core)
    owner_chip, owner_core = owners // 2, owners % 2

    def one():
        core = jnp.sum(jnp.where(owner_chip == chip, owner_core, 0))
        plane = lax.dynamic_index_in_dim(planes, core, 0, keepdims=False)
        tiles = plane.reshape(rows, chips, cols // chips).transpose(1, 0, 2)
        tiles = lax.all_to_all(tiles, "ang", 0, 0, tiled=True, axis_index_groups=by_chip)
        return tuple(lax.dynamic_index_in_dim(tiles, c, 0, keepdims=False) for c in owner_chip)

    def both():
        tiles = planes.reshape(2, rows, chips, cols // chips).transpose(2, 0, 1, 3)
        tiles = lax.all_to_all(tiles, "ang", 0, 0, tiled=True, axis_index_groups=by_chip)
        tiles = tiles.reshape(angs, rows, cols // chips)
        return tuple(lax.dynamic_index_in_dim(tiles, o, 0, keepdims=False) for o in owners)

    shared = (owner_chip[:, None] == owner_chip[None, :]).sum() > owners.shape[0]
    return lax.cond(shared, both, one)


def per_device(contrast, owners, tilts):
    depth, rows, cols = contrast.shape[1:]
    slabs = owners.shape[0]
    spots = lax.axis_size("xy")
    ang = lax.axis_index("ang")
    spot = lax.axis_index("xy")
    angs = lax.axis_size("ang")

    kept = keep(contrast[0], owners)

    tails = jnp.concatenate([kept[k][rows - HALO[k] :] for k in range(slabs)], axis=0)
    heads = jnp.concatenate([kept[k][: HALO[k]] for k in range(slabs)], axis=0)
    above = lax.ppermute(tails, "xy", [(i, i + 1) for i in range(spots - 1)])
    below = lax.ppermute(heads, "xy", [(i + 1, i) for i in range(spots - 1)])

    columns = [[4 * z + q for z in range(angs // 4)] for q in range(4)]
    swap_x = [(i, i ^ 2) for i in range(angs)]
    swap_core = [(i, i ^ 1) for i in range(angs)]

    def along_z(chosen, after=None):
        parts = []
        for k in chosen:
            at = slice(sum(HALO[:k]), sum(HALO[: k + 1]))
            parts += [above[at], kept[k], below[at]]
        piece = jnp.concatenate(parts, axis=0)
        if after is not None:
            piece, after = lax.optimization_barrier((piece, after))
        copies = jnp.broadcast_to(piece, (angs // 4,) + piece.shape)
        return lax.all_to_all(copies, "ang", 0, 0, tiled=True, axis_index_groups=columns)

    def from_core(mine, other):
        return lax.ppermute(jnp.stack([mine, other]), "ang", swap_core)

    early, late = (0, 1), (2,)
    mine = along_z(early)
    other = lax.ppermute(mine, "ang", swap_x)
    late_mine = along_z(late, mine)
    late_mine, other, tilts = lax.optimization_barrier((late_mine, other, tilts))
    late_other = lax.ppermute(late_mine, "ang", swap_x)
    first = mine, other, from_core(mine, other)

    wave = waves(tilts, spot * rows, rows * spots, cols)
    place = jnp.stack([ang // 2 % 2, ang % 2, spot, jnp.int32(spots - 1)])

    def step(slab, before, pieces):
        start, end = slab == 0, slab == slabs - 1
        state = jax.ShapeDtypeStruct((2, ROWS, cols), jnp.float32)
        out = jax.ShapeDtypeStruct((1, rows, cols), jnp.float32)
        in_vmem = pl.BlockSpec(memory_space=pltpu.VMEM)
        return pl.pallas_call(
            functools.partial(
                through,
                slab=slab,
                skip=sum(rows + 2 * HALO[k] for k in early if k < slab) if slab in early else 0,
                cols=cols // LANES,
                first=start,
                last=end,
            ),
            out_shape=(out, out) if end else state,
            in_specs=[pl.BlockSpec(memory_space=pltpu.SMEM)] + [in_vmem] * (len(before) + len(pieces)),
            out_specs=(in_vmem, in_vmem) if end else in_vmem,
            scratch_shapes=[
                pltpu.VMEM((depth, ROWS, cols), jnp.float32),
                pltpu.VMEM(state.shape, jnp.float32),
                pltpu.VMEM(state.shape, jnp.float32),
            ],
            compiler_params=pltpu.CompilerParams(vmem_limit_bytes=32 * 1024 * 1024),
            cost_estimate=pl.CostEstimate(flops=20_000_000, bytes_accessed=6_000_000, transcendentals=0),
        )(place, *before, *pieces)

    field = step(1, (step(0, wave, first),), first)
    late_other, field = lax.optimization_barrier((late_other, field))
    return step(2, (field,), (late_mine, late_other, from_core(late_mine, late_other)))


def solution(mesh):
    placed = (P("ang", None, "xy", None), P(), P("ang", None))
    return jax.shard_map(
        per_device,
        mesh=mesh,
        in_specs=placed,
        out_specs=(P("ang", "xy", None), P("ang", "xy", None)),
        check_vma=False,
    )
```

```python
import functools
import math

import jax
import jax.numpy as jnp
from jax import lax
from jax.experimental import pallas as pl
from jax.experimental.pallas import tpu as pltpu
from jax.sharding import PartitionSpec as P

diffraction = 0.05
phase_gain = 0.08

HALO = (12, 8, 4)
TOP = 24
ROWS = 112
LANES = 128

TRIAL = ((1, 13), (1, 13), (2, 12), (2, 12), (2, 12), (2, 12))
FIELD = ((1, 13), (2, 12), (2, 12), (2, 12), (2, 12), (3, 11))


def neighbours(tile, above, below, cols, row, lane):
    sums = []
    for c in range(cols):
        here = tile[c]
        zero = jnp.zeros_like(here)
        west = tile[c - 1] if c else zero
        east = tile[c + 1] if c < cols - 1 else zero
        up = pltpu.roll(jnp.where(row == 7, above[c], here), 1, 0)
        down = pltpu.roll(jnp.where(row == 0, below[c], here), 7, 0)
        left = pltpu.roll(jnp.where(lane == LANES - 1, west, here), 1, 1)
        right = pltpu.roll(jnp.where(lane == 0, east, here), LANES - 1, 1)
        sums.append((up + down) + (left + right))
    return sums


def load(ref, part, i, cols):
    at = pl.ds(pl.multiple_of(i * 8, 8), 8)
    return [ref[part, at, c * LANES : (c + 1) * LANES] for c in range(cols)]


def coupled(ref, part, i, plane, cols, row, lane):
    here = load(ref, part, i, cols)
    around = neighbours(here, load(ref, part, i - 1, cols), load(ref, part, i + 1, cols), cols, row, lane)
    return here, [s + p * h for s, p, h in zip(around, plane, here)]


def assemble(place, own, others, planes, slab, skip, cols):
    halo = HALO[slab]
    half = 32

    def put(ref, core):
        for z in range(cols // 2):
            for q in range(2):
                column = place[0] if q == 0 else 1 - place[0]
                at = pl.ds(pl.multiple_of((2 * z + column) * LANES, LANES), LANES)
                for j in range(2):
                    for first, count, to in (
                        (skip + half * j, half, TOP + half * core),
                        (skip + 2 * half + halo * j, halo, TOP + 2 * half if core else TOP - halo),
                    ):
                        values = ref[q][z, first : first + count, :]
                        planes[j, to : to + count, at] = (phase_gain / diffraction) * values - 4.0

    for core in range(2):

        @pl.when(place[1] == core)
        def _():
            put(own, core)
            put(others, 1 - core)


def clear_outside(place, parts):
    @pl.when(place[2] == 0)
    def _():
        for ref in parts:
            ref[0:TOP, :] = jnp.zeros((TOP, ref.shape[1]), jnp.float32)

    @pl.when(place[2] == place[3])
    def _():
        for ref in parts:
            ref[TOP + 64 : ROWS, :] = jnp.zeros((ROWS - TOP - 64, ref.shape[1]), jnp.float32)


def advance(place, s, plane_ref, field, trial, after, cols):
    row = lax.broadcasted_iota(jnp.int32, (8, LANES), 0)
    lane = lax.broadcasted_iota(jnp.int32, (8, LANES), 1)

    def first(i, carry):
        at = pl.ds(pl.multiple_of(i * 8, 8), 8)
        plane = [plane_ref[at, c * LANES : (c + 1) * LANES] for c in range(cols)]
        re, a = coupled(field, 0, i, plane, cols, row, lane)
        for c in range(cols):
            span = slice(c * LANES, (c + 1) * LANES)
            trial[1, at, span] = field[1, at, span] + diffraction * a[c]
        im, b = coupled(field, 1, i, plane, cols, row, lane)
        for c in range(cols):
            span = slice(c * LANES, (c + 1) * LANES)
            trial[0, at, span] = re[c] - diffraction * b[c]
        return carry

    def second(i, carry):
        at = pl.ds(pl.multiple_of(i * 8, 8), 8)
        to = pl.ds(pl.multiple_of((i - after[1]) * 8, 8), 8)
        plane = [plane_ref[at, c * LANES : (c + 1) * LANES] for c in range(cols)]
        re, a = coupled(trial, 0, i, plane, cols, row, lane)
        for c in range(cols):
            span = slice(c * LANES, (c + 1) * LANES)
            old = field[1, at, span] + trial[1, at, span]
            after[0][1][to, span] = 0.5 * old + (0.5 * diffraction) * a[c]
        im, b = coupled(trial, 1, i, plane, cols, row, lane)
        for c in range(cols):
            span = slice(c * LANES, (c + 1) * LANES)
            old = field[0, at, span] + re[c]
            after[0][0][to, span] = 0.5 * old - (0.5 * diffraction) * b[c]
        return carry

    lax.fori_loop(*TRIAL[s], first, 0, unroll=True)
    clear_outside(place, (trial.at[0], trial.at[1]))
    lax.fori_loop(*FIELD[s], second, 0, unroll=True)


def incident(rowwave, colwave, field, cols):
    def start(i, carry):
        at = pl.ds(pl.multiple_of(i * 8, 8), 8)
        c_row, s_row = rowwave[0, at, :], rowwave[1, at, :]
        for c in range(cols):
            span = slice(c * LANES, (c + 1) * LANES)
            c_col, s_col = colwave[0, :, span], colwave[1, :, span]
            field[0, at, span] = c_row * c_col - s_row * s_col
            field[1, at, span] = s_row * c_col + c_row * s_col
        return carry

    lax.fori_loop(0, ROWS // 8, start, 0, unroll=2)


def through(*refs, slab, skip, cols, first, last):
    refs = list(refs)
    place = refs.pop(0)
    waves = [refs.pop(0) for _ in range(2)] if first else []
    before = None if first else refs.pop(0)
    mine, other, theirs = refs[:3]
    planes, trial, field = refs[-3:]
    assemble(place, (mine, other), (theirs.at[0], theirs.at[1]), planes, slab, skip, cols)
    if first:
        incident(*waves, field, cols)
        before = field
    middle = field.at[0], field.at[1]
    advance(place, 2 * slab, planes.at[0], before, trial, (middle, 0), cols)
    clear_outside(place, middle)
    if last:
        advance(place, 2 * slab + 1, planes.at[1], field, trial, ((refs[3].at[0], refs[4].at[0]), TOP // 8), cols)
    else:
        after = refs[3].at[0], refs[3].at[1]
        advance(place, 2 * slab + 1, planes.at[1], field, trial, (after, 0), cols)
        clear_outside(place, after)


def waves(tilts, anchor, total_rows, cols):
    row_ids = anchor - TOP + jnp.arange(ROWS, dtype=jnp.int32)
    col_ids = jnp.arange(cols, dtype=jnp.int32)
    along_rows = (tilts[0, 0] * row_ids) % total_rows
    along_cols = (tilts[0, 1] * col_ids) % cols
    row_angle = 2.0 * math.pi * (along_rows.astype(jnp.float32) / total_rows)
    col_angle = 2.0 * math.pi * (along_cols.astype(jnp.float32) / cols)
    inside = (row_ids >= 0) & (row_ids < total_rows)
    by_row = jnp.where(inside, jnp.stack([jnp.cos(row_angle), jnp.sin(row_angle)]), 0.0)
    by_col = jnp.stack([jnp.cos(col_angle), jnp.sin(col_angle)])
    return (
        jnp.broadcast_to(by_row[:, :, None], (2, ROWS, LANES)),
        jnp.broadcast_to(by_col[:, None, :], (2, 8, cols)),
    )


def keep(contrast, owners):
    depth, rows, cols = contrast.shape
    angs = lax.axis_size("ang")
    chips = angs // 2
    chip = lax.axis_index("ang") // 2
    by_chip = [[2 * i + c for i in range(chips)] for c in range(2)]
    by_core = [[2 * i, 2 * i + 1] for i in range(chips)]
    halves = contrast.reshape(depth, 2, rows // 2, cols).transpose(1, 0, 2, 3).reshape(2, rows, cols)
    halves = lax.all_to_all(halves, "ang", 0, 0, tiled=True, axis_index_groups=by_core)
    owner_chip, owner_core = owners // 2, owners % 2
    core = jnp.sum(jnp.where(owner_chip == chip, owner_core, 0))
    shared = (owner_chip[:, None] == owner_chip[None, :]).sum() > owners.shape[0]
    halves, core, shared = lax.optimization_barrier((halves, core, shared))

    def at(tiles, i):
        return lax.dynamic_index_in_dim(tiles, i, 0, keepdims=False, allow_negative_indices=False)

    def one():
        half = jnp.where(core == 1, halves[1], halves[0])
        tiles = half.reshape(rows, chips, cols // chips).transpose(1, 0, 2)
        tiles = lax.all_to_all(tiles, "ang", 0, 0, tiled=True, axis_index_groups=by_chip)
        return tuple(at(tiles, c) for c in owner_chip)

    def both():
        tiles = halves.reshape(2, rows, chips, cols // chips).transpose(2, 0, 1, 3)
        tiles = lax.all_to_all(tiles, "ang", 0, 0, tiled=True, axis_index_groups=by_chip)
        tiles = tiles.reshape(angs, rows, cols // chips)
        return tuple(at(tiles, o) for o in owners)

    return lax.cond(shared, both, one)


def per_device(contrast, owners, tilts):
    depth, rows, cols = contrast.shape[1:]
    slabs = owners.shape[0]
    spots = lax.axis_size("xy")
    ang = lax.axis_index("ang")
    spot = lax.axis_index("xy")
    angs = lax.axis_size("ang")

    kept = keep(contrast[0], owners)

    half = rows // 2
    heads = [kept[k][half * j : half * j + HALO[k]] for k in range(slabs) for j in range(depth)]
    tails = [kept[k][half * (j + 1) - HALO[k] : half * (j + 1)] for k in range(slabs) for j in range(depth)]
    edge = jnp.where(ang % 2 == 0, jnp.concatenate(heads, axis=0), jnp.concatenate(tails, axis=0))
    up = [(spots * a + i, spots * (a + 1) + i - 1) for a in range(0, angs, 2) for i in range(1, spots)]
    edge = lax.ppermute(edge, ("ang", "xy"), up + [(j, i) for i, j in up])

    tilts, kept = lax.optimization_barrier((tilts, kept))
    wave = waves(tilts, spot * rows, rows * spots, cols)
    edge, wave = lax.optimization_barrier((edge, wave))

    columns = [[4 * z + q for z in range(angs // 4)] for q in range(4)]
    swap_x = [(i, i ^ 2) for i in range(angs)]
    swap_core = [(i, i ^ 1) for i in range(angs)]

    def along_z(chosen, after=None):
        parts = []
        for k in chosen:
            parts += [kept[k], edge[depth * sum(HALO[:k]) : depth * sum(HALO[: k + 1])]]
        piece = jnp.concatenate(parts, axis=0)
        if after is not None:
            piece, after = lax.optimization_barrier((piece, after))
        copies = jnp.broadcast_to(piece, (angs // 4,) + piece.shape)
        return lax.all_to_all(copies, "ang", 0, 0, tiled=True, axis_index_groups=columns)

    def from_core(mine, other):
        return lax.ppermute(jnp.stack([mine, other]), "ang", swap_core)

    early, late = (0, 1), (2,)
    mine = along_z(early)
    other = lax.ppermute(mine, "ang", swap_x)
    late_mine = along_z(late, mine)
    late_mine, other = lax.optimization_barrier((late_mine, other))
    late_other = lax.ppermute(late_mine, "ang", swap_x)
    first = mine, other, from_core(mine, other)

    place = jnp.stack([ang // 2 % 2, ang % 2, spot, jnp.int32(spots - 1)])

    def step(slab, before, pieces):
        start, end = slab == 0, slab == slabs - 1
        state = jax.ShapeDtypeStruct((2, ROWS, cols), jnp.float32)
        out = jax.ShapeDtypeStruct((1, rows, cols), jnp.float32)
        in_vmem = pl.BlockSpec(memory_space=pltpu.VMEM)
        return pl.pallas_call(
            functools.partial(
                through,
                slab=slab,
                skip=sum(rows + 2 * HALO[k] for k in early if k < slab) if slab in early else 0,
                cols=cols // LANES,
                first=start,
                last=end,
            ),
            out_shape=(out, out) if end else state,
            in_specs=[pl.BlockSpec(memory_space=pltpu.SMEM)] + [in_vmem] * (len(before) + len(pieces)),
            out_specs=(in_vmem, in_vmem) if end else in_vmem,
            scratch_shapes=[
                pltpu.VMEM((depth, ROWS, cols), jnp.float32),
                pltpu.VMEM(state.shape, jnp.float32),
                pltpu.VMEM(state.shape, jnp.float32),
            ],
            compiler_params=pltpu.CompilerParams(vmem_limit_bytes=32 * 1024 * 1024),
            cost_estimate=pl.CostEstimate(flops=20_000_000, bytes_accessed=6_000_000, transcendentals=0),
        )(place, *before, *pieces)

    field = step(1, (step(0, wave, first),), first)
    late_other, field = lax.optimization_barrier((late_other, field))
    return step(2, (field,), (late_mine, late_other, from_core(late_mine, late_other)))


def solution(mesh):
    placed = (P("ang", None, "xy", None), P(), P("ang", None))
    return jax.shard_map(
        per_device,
        mesh=mesh,
        in_specs=placed,
        out_specs=(P("ang", "xy", None), P("ang", "xy", None)),
        check_vma=False,
    )
```

```python
import functools
import math

import jax
import jax.numpy as jnp
from jax import lax
from jax.experimental import pallas as pl
from jax.experimental.pallas import tpu as pltpu
from jax.sharding import PartitionSpec as P

diffraction = 0.05
phase_gain = 0.08

HALO = (11, 9, 7, 5, 3, 1)
TOP = 24
ROWS = 112
LANES = 128

TRIAL = ((1, 13), (1, 13), (2, 12), (2, 12), (2, 12), (2, 12))
FIELD = ((1, 13), (2, 12), (2, 12), (2, 12), (2, 12), (3, 11))


def neighbours(tile, above, below, cols, row, lane):
    sums = []
    for c in range(cols):
        here = tile[c]
        zero = jnp.zeros_like(here)
        west = tile[c - 1] if c else zero
        east = tile[c + 1] if c < cols - 1 else zero
        up = pltpu.roll(jnp.where(row == 7, above[c], here), 1, 0)
        down = pltpu.roll(jnp.where(row == 0, below[c], here), 7, 0)
        left = pltpu.roll(jnp.where(lane == LANES - 1, west, here), 1, 1)
        right = pltpu.roll(jnp.where(lane == 0, east, here), LANES - 1, 1)
        sums.append((up + down) + (left + right))
    return sums


def load(ref, part, i, cols):
    at = pl.ds(pl.multiple_of(i * 8, 8), 8)
    return [ref[part, at, c * LANES : (c + 1) * LANES] for c in range(cols)]


def coupled(ref, part, i, plane, cols, row, lane):
    here = load(ref, part, i, cols)
    around = neighbours(here, load(ref, part, i - 1, cols), load(ref, part, i + 1, cols), cols, row, lane)
    return here, [s + p * h for s, p, h in zip(around, plane, here)]


def assemble(place, own, others, planes, slab, place_in, cols):
    half = 32

    def put(ref, core):
        for z in range(cols // 2):
            for q in range(2):
                column = place[0] if q == 0 else 1 - place[0]
                at = pl.ds(pl.multiple_of((2 * z + column) * LANES, LANES), LANES)
                rim = place_in[1]
                for j in range(2):
                    halo = HALO[2 * slab + j]
                    for first, count, to in (
                        (place_in[0] + half * j, half, TOP + half * core),
                        (rim, halo, TOP + 2 * half if core else TOP - halo),
                    ):
                        values = ref[q][z, first : first + count, :]
                        planes[j, to : to + count, at] = (phase_gain / diffraction) * values - 4.0
                    rim += halo

    for core in range(2):

        @pl.when(place[1] == core)
        def _():
            put(own, core)
            put(others, 1 - core)


def clear_outside(place, parts):
    @pl.when(place[2] == 0)
    def _():
        for ref in parts:
            ref[0:TOP, :] = jnp.zeros((TOP, ref.shape[1]), jnp.float32)

    @pl.when(place[2] == place[3])
    def _():
        for ref in parts:
            ref[TOP + 64 : ROWS, :] = jnp.zeros((ROWS - TOP - 64, ref.shape[1]), jnp.float32)


def advance(place, s, plane_ref, field, trial, after, cols):
    row = lax.broadcasted_iota(jnp.int32, (8, LANES), 0)
    lane = lax.broadcasted_iota(jnp.int32, (8, LANES), 1)

    def first(i, carry):
        at = pl.ds(pl.multiple_of(i * 8, 8), 8)
        plane = [plane_ref[at, c * LANES : (c + 1) * LANES] for c in range(cols)]
        re, a = coupled(field, 0, i, plane, cols, row, lane)
        for c in range(cols):
            span = slice(c * LANES, (c + 1) * LANES)
            trial[1, at, span] = field[1, at, span] + diffraction * a[c]
        im, b = coupled(field, 1, i, plane, cols, row, lane)
        for c in range(cols):
            span = slice(c * LANES, (c + 1) * LANES)
            trial[0, at, span] = re[c] - diffraction * b[c]
        return carry

    def second(i, carry):
        at = pl.ds(pl.multiple_of(i * 8, 8), 8)
        to = pl.ds(pl.multiple_of((i - after[1]) * 8, 8), 8)
        plane = [plane_ref[at, c * LANES : (c + 1) * LANES] for c in range(cols)]
        re, a = coupled(trial, 0, i, plane, cols, row, lane)
        for c in range(cols):
            span = slice(c * LANES, (c + 1) * LANES)
            old = field[1, at, span] + trial[1, at, span]
            after[0][1][to, span] = 0.5 * old + (0.5 * diffraction) * a[c]
        im, b = coupled(trial, 1, i, plane, cols, row, lane)
        for c in range(cols):
            span = slice(c * LANES, (c + 1) * LANES)
            old = field[0, at, span] + re[c]
            after[0][0][to, span] = 0.5 * old - (0.5 * diffraction) * b[c]
        return carry

    lax.fori_loop(*TRIAL[s], first, 0, unroll=True)
    clear_outside(place, (trial.at[0], trial.at[1]))
    lax.fori_loop(*FIELD[s], second, 0, unroll=True)


def incident(rowwave, colwave, field, cols):
    def start(i, carry):
        at = pl.ds(pl.multiple_of(i * 8, 8), 8)
        c_row, s_row = rowwave[0, at, :], rowwave[1, at, :]
        for c in range(cols):
            span = slice(c * LANES, (c + 1) * LANES)
            c_col, s_col = colwave[0, :, span], colwave[1, :, span]
            field[0, at, span] = c_row * c_col - s_row * s_col
            field[1, at, span] = s_row * c_col + c_row * s_col
        return carry

    lax.fori_loop(0, ROWS // 8, start, 0, unroll=2)


def through(*refs, slab, place_in, cols, first, last):
    refs = list(refs)
    place = refs.pop(0)
    waves = [refs.pop(0) for _ in range(2)] if first else []
    before = None if first else refs.pop(0)
    mine, other, theirs = refs[:3]
    planes, trial, field = refs[-3:]
    assemble(place, (mine, other), (theirs.at[0], theirs.at[1]), planes, slab, place_in, cols)
    if first:
        incident(*waves, field, cols)
        before = field
    middle = field.at[0], field.at[1]
    advance(place, 2 * slab, planes.at[0], before, trial, (middle, 0), cols)
    clear_outside(place, middle)
    if last:
        advance(place, 2 * slab + 1, planes.at[1], field, trial, ((refs[3].at[0], refs[4].at[0]), TOP // 8), cols)
    else:
        after = refs[3].at[0], refs[3].at[1]
        advance(place, 2 * slab + 1, planes.at[1], field, trial, (after, 0), cols)
        clear_outside(place, after)


def waves(tilts, anchor, total_rows, cols):
    row_ids = anchor - TOP + jnp.arange(ROWS, dtype=jnp.int32)
    col_ids = jnp.arange(cols, dtype=jnp.int32)
    along_rows = (tilts[0, 0] * row_ids) % total_rows
    along_cols = (tilts[0, 1] * col_ids) % cols
    row_angle = 2.0 * math.pi * (along_rows.astype(jnp.float32) / total_rows)
    col_angle = 2.0 * math.pi * (along_cols.astype(jnp.float32) / cols)
    inside = (row_ids >= 0) & (row_ids < total_rows)
    by_row = jnp.where(inside, jnp.stack([jnp.cos(row_angle), jnp.sin(row_angle)]), 0.0)
    by_col = jnp.stack([jnp.cos(col_angle), jnp.sin(col_angle)])
    return (
        jnp.broadcast_to(by_row[:, :, None], (2, ROWS, LANES)),
        jnp.broadcast_to(by_col[:, None, :], (2, 8, cols)),
    )


def keep(contrast, owners, wave):
    depth, rows, cols = contrast.shape
    angs = lax.axis_size("ang")
    chips = angs // 2
    chip = lax.axis_index("ang") // 2
    by_chip = [[2 * i + c for i in range(chips)] for c in range(2)]
    first = lax.axis_index("ang") % 2 == 0
    top, bottom = contrast[:, : rows // 2], contrast[:, rows // 2 :]
    given = jnp.where(first, bottom, top)
    got = lax.ppermute(given, "ang", [(i, i ^ 1) for i in range(angs)])
    owner_chip, owner_core = owners // 2, owners % 2
    core = jnp.sum(jnp.where(owner_chip == chip, owner_core, 0))
    shared = (owner_chip[:, None] == owner_chip[None, :]).sum() > owners.shape[0]
    got, core, shared = lax.optimization_barrier((got, core, shared))
    def at(tiles, i):
        return lax.dynamic_index_in_dim(tiles, i, 0, keepdims=False)

    def one():
        kept = jnp.where(first, top, bottom)
        half = jnp.where((core == 0) == first, kept, got)
        tiles = half.reshape(rows, chips, cols // chips).transpose(1, 0, 2)
        tiles = lax.all_to_all(tiles, "ang", 0, 0, tiled=True, axis_index_groups=by_chip)
        return tuple(at(tiles, c) for c in owner_chip), wave()

    def both():
        halves = jnp.stack([jnp.where(first, top, got), jnp.where(first, got, bottom)])
        tiles = halves.reshape(2, rows, chips, cols // chips).transpose(2, 0, 1, 3)
        tiles = lax.all_to_all(tiles, "ang", 0, 0, tiled=True, axis_index_groups=by_chip)
        tiles = tiles.reshape(angs, rows, cols // chips)
        return tuple(at(tiles, o) for o in owners), wave()

    return lax.cond(shared, both, one)


def per_device(contrast, owners, tilts):
    depth, rows, cols = contrast.shape[1:]
    slabs = owners.shape[0]
    spots = lax.axis_size("xy")
    ang = lax.axis_index("ang")
    spot = lax.axis_index("xy")
    angs = lax.axis_size("ang")

    kept, wave = keep(contrast[0], owners, lambda: waves(tilts, spot * rows, rows * spots, cols))

    half = rows // 2
    slices = [(k, j, HALO[depth * k + j]) for k in range(slabs) for j in range(depth)]
    heads = [kept[k][half * j : half * j + halo] for k, j, halo in slices]
    tails = [kept[k][half * (j + 1) - halo : half * (j + 1)] for k, j, halo in slices]
    edge = jnp.where(ang % 2 == 0, jnp.concatenate(heads, axis=0), jnp.concatenate(tails, axis=0))
    up = [(spots * a + i, spots * (a + 1) + i - 1) for a in range(0, angs, 2) for i in range(1, spots)]
    edge = lax.ppermute(edge, ("ang", "xy"), up + [(j, i) for i, j in up])

    columns = [[4 * z + q for z in range(angs // 4)] for q in range(4)]
    swap_x = [(i, i ^ 2) for i in range(angs)]
    swap_core = [(i, i ^ 1) for i in range(angs)]

    def along_z(chosen, after=None):
        rims = [edge[sum(HALO[: depth * k]) : sum(HALO[: depth * (k + 1)])] for k in chosen]
        spare = jnp.zeros((-sum(r.shape[0] for r in rims) % 8, cols // (angs // 2)), jnp.float32)
        piece = jnp.concatenate([kept[k] for k in chosen] + rims + [spare], axis=0)
        if after is not None:
            piece, after = lax.optimization_barrier((piece, after))
        copies = jnp.broadcast_to(piece, (angs // 4,) + piece.shape)
        return lax.all_to_all(copies, "ang", 0, 0, tiled=True, axis_index_groups=columns)

    def from_core(mine, other):
        return lax.ppermute(jnp.stack([mine, other]), "ang", swap_core)

    early, late = (0, 1), (2,)
    mine = along_z(early)
    other = lax.ppermute(mine, "ang", swap_x)
    late_mine = along_z(late, mine)
    late_mine, other = lax.optimization_barrier((late_mine, other))
    late_other = lax.ppermute(late_mine, "ang", swap_x)
    first = mine, other, from_core(mine, other)

    place = jnp.stack([ang // 2 % 2, ang % 2, spot, jnp.int32(spots - 1)])

    def step(slab, before, pieces):
        start, end = slab == 0, slab == slabs - 1
        chosen = early if slab in early else late
        state = jax.ShapeDtypeStruct((2, ROWS, cols), jnp.float32)
        out = jax.ShapeDtypeStruct((1, rows, cols), jnp.float32)
        in_vmem = pl.BlockSpec(memory_space=pltpu.VMEM)
        return pl.pallas_call(
            functools.partial(
                through,
                slab=slab,
                place_in=(rows * chosen.index(slab), rows * len(chosen) + sum(HALO[depth * chosen[0] : depth * slab])),
                cols=cols // LANES,
                first=start,
                last=end,
            ),
            out_shape=(out, out) if end else state,
            in_specs=[pl.BlockSpec(memory_space=pltpu.SMEM)] + [in_vmem] * (len(before) + len(pieces)),
            out_specs=(in_vmem, in_vmem) if end else in_vmem,
            scratch_shapes=[
                pltpu.VMEM((depth, ROWS, cols), jnp.float32),
                pltpu.VMEM(state.shape, jnp.float32),
                pltpu.VMEM(state.shape, jnp.float32),
            ],
            compiler_params=pltpu.CompilerParams(vmem_limit_bytes=32 * 1024 * 1024),
            cost_estimate=pl.CostEstimate(flops=20_000_000, bytes_accessed=6_000_000, transcendentals=0),
        )(place, *before, *pieces)

    field = step(1, (step(0, wave, first),), first)
    late_other, field = lax.optimization_barrier((late_other, field))
    return step(2, (field,), (late_mine, late_other, from_core(late_mine, late_other)))


def solution(mesh):
    placed = (P("ang", None, "xy", None), P(), P("ang", None))
    return jax.shard_map(
        per_device,
        mesh=mesh,
        in_specs=placed,
        out_specs=(P("ang", "xy", None), P("ang", "xy", None)),
        check_vma=False,
    )
```

```python
import functools
import math

import jax
import jax.numpy as jnp
from jax import lax
from jax.experimental import pallas as pl
from jax.experimental.pallas import tpu as pltpu
from jax.sharding import PartitionSpec as P

diffraction = 0.05
phase_gain = 0.08

HALO = (11, 9, 7, 5, 3, 1)
TOP = 24
ROWS = 112
LANES = 128

TRIAL = ((1, 13), (1, 13), (2, 12), (2, 12), (2, 12), (2, 12))
FIELD = ((1, 13), (2, 12), (2, 12), (2, 12), (2, 12), (3, 11))


def neighbours(tile, above, below, cols, row, lane):
    sums = []
    for c in range(cols):
        here = tile[c]
        zero = jnp.zeros_like(here)
        west = tile[c - 1] if c else zero
        east = tile[c + 1] if c < cols - 1 else zero
        up = pltpu.roll(jnp.where(row == 7, above[c], here), 1, 0)
        down = pltpu.roll(jnp.where(row == 0, below[c], here), 7, 0)
        left = pltpu.roll(jnp.where(lane == LANES - 1, west, here), 1, 1)
        right = pltpu.roll(jnp.where(lane == 0, east, here), LANES - 1, 1)
        sums.append((up + down) + (left + right))
    return sums


def load(ref, part, i, cols):
    at = pl.ds(pl.multiple_of(i * 8, 8), 8)
    return [ref[part, at, c * LANES : (c + 1) * LANES] for c in range(cols)]


def coupled(ref, part, i, plane, cols, row, lane):
    here = load(ref, part, i, cols)
    around = neighbours(here, load(ref, part, i - 1, cols), load(ref, part, i + 1, cols), cols, row, lane)
    return here, [s + p * h for s, p, h in zip(around, plane, here)]


def assemble(place, own, others, planes, slab, place_in, cols):
    half = 32

    def put(ref, core):
        for z in range(cols // 2):
            for q in range(2):
                column = place[0] if q == 0 else 1 - place[0]
                at = pl.ds(pl.multiple_of((2 * z + column) * LANES, LANES), LANES)
                rim = place_in[1]
                for j in range(2):
                    halo = HALO[2 * slab + j]
                    for first, count, to in (
                        (place_in[0] + half * j, half, TOP + half * core),
                        (rim, halo, TOP + 2 * half if core else TOP - halo),
                    ):
                        values = ref[q][z, first : first + count, :]
                        planes[j, to : to + count, at] = (phase_gain / diffraction) * values - 4.0
                    rim += halo

    for core in range(2):

        @pl.when(place[1] == core)
        def _():
            put(own, core)
            put(others, 1 - core)


def clear_outside(place, parts):
    @pl.when(place[2] == 0)
    def _():
        for ref in parts:
            ref[0:TOP, :] = jnp.zeros((TOP, ref.shape[1]), jnp.float32)

    @pl.when(place[2] == place[3])
    def _():
        for ref in parts:
            ref[TOP + 64 : ROWS, :] = jnp.zeros((ROWS - TOP - 64, ref.shape[1]), jnp.float32)


def advance(place, s, plane_ref, field, trial, after, cols, done=None):
    row = lax.broadcasted_iota(jnp.int32, (8, LANES), 0)
    lane = lax.broadcasted_iota(jnp.int32, (8, LANES), 1)

    def first(i, carry):
        at = pl.ds(pl.multiple_of(i * 8, 8), 8)
        plane = [plane_ref[at, c * LANES : (c + 1) * LANES] for c in range(cols)]
        re, a = coupled(field, 0, i, plane, cols, row, lane)
        for c in range(cols):
            span = slice(c * LANES, (c + 1) * LANES)
            trial[1, at, span] = field[1, at, span] + diffraction * a[c]
        im, b = coupled(field, 1, i, plane, cols, row, lane)
        for c in range(cols):
            span = slice(c * LANES, (c + 1) * LANES)
            trial[0, at, span] = re[c] - diffraction * b[c]
        return carry

    def second(i, carry):
        at = pl.ds(pl.multiple_of(i * 8, 8), 8)
        to = pl.ds(pl.multiple_of((i - after[1]) * 8, 8), 8)
        plane = [plane_ref[at, c * LANES : (c + 1) * LANES] for c in range(cols)]
        re, a = coupled(trial, 0, i, plane, cols, row, lane)
        for c in range(cols):
            span = slice(c * LANES, (c + 1) * LANES)
            old = field[1, at, span] + trial[1, at, span]
            after[0][1][to, span] = 0.5 * old + (0.5 * diffraction) * a[c]
        im, b = coupled(trial, 1, i, plane, cols, row, lane)
        for c in range(cols):
            span = slice(c * LANES, (c + 1) * LANES)
            old = field[0, at, span] + re[c]
            after[0][0][to, span] = 0.5 * old - (0.5 * diffraction) * b[c]
        if done is not None:
            done(i - after[1])
        return carry

    lax.fori_loop(*TRIAL[s], first, 0, unroll=True)
    clear_outside(place, (trial.at[0], trial.at[1]))
    lax.fori_loop(*FIELD[s], second, 0, unroll=True)


def incident(rowwave, colwave, field, cols):
    def start(i, carry):
        at = pl.ds(pl.multiple_of(i * 8, 8), 8)
        c_row, s_row = rowwave[0, at, :], rowwave[1, at, :]
        for c in range(cols):
            span = slice(c * LANES, (c + 1) * LANES)
            c_col, s_col = colwave[0, :, span], colwave[1, :, span]
            field[0, at, span] = c_row * c_col - s_row * s_col
            field[1, at, span] = s_row * c_col + c_row * s_col
        return carry

    lax.fori_loop(0, ROWS // 8, start, 0, unroll=2)


def through(*refs, slab, place_in, cols, first, last):
    refs = list(refs)
    place = refs.pop(0)
    waves = [refs.pop(0) for _ in range(2)] if first else []
    before = None if first else refs.pop(0)
    mine, other, theirs = refs[:3]
    sent, exits = (refs.pop(), refs.pop()) if last else (None, None)
    planes, trial, field = refs[-3:]
    assemble(place, (mine, other), (theirs.at[0], theirs.at[1]), planes, slab, place_in, cols)
    if first:
        incident(*waves, field, cols)
        before = field
    middle = field.at[0], field.at[1]
    advance(place, 2 * slab, planes.at[0], before, trial, (middle, 0), cols)
    clear_outside(place, middle)
    if last:

        def copies(i):
            at = pl.ds(pl.multiple_of(i * 8, 8), 8)
            return [
                pltpu.make_async_copy(exits.at[part, at, :], refs[3 + part].at[0, at, :], sent.at[part, i])
                for part in range(2)
            ]

        def done(i):
            for copy in copies(i):
                copy.start()

        advance(place, 2 * slab + 1, planes.at[1], field, trial, ((exits.at[0], exits.at[1]), TOP // 8), cols, done)
        for i in range(8):
            for copy in copies(i):
                copy.wait()
    else:
        after = refs[3].at[0], refs[3].at[1]
        advance(place, 2 * slab + 1, planes.at[1], field, trial, (after, 0), cols)
        clear_outside(place, after)


def waves(tilts, anchor, total_rows, cols):
    row_ids = anchor - TOP + jnp.arange(ROWS, dtype=jnp.int32)
    col_ids = jnp.arange(cols, dtype=jnp.int32)
    along_rows = (tilts[0, 0] * row_ids) % total_rows
    along_cols = (tilts[0, 1] * col_ids) % cols
    row_angle = 2.0 * math.pi * (along_rows.astype(jnp.float32) / total_rows)
    col_angle = 2.0 * math.pi * (along_cols.astype(jnp.float32) / cols)
    inside = (row_ids >= 0) & (row_ids < total_rows)
    by_row = jnp.where(inside, jnp.stack([jnp.cos(row_angle), jnp.sin(row_angle)]), 0.0)
    by_col = jnp.stack([jnp.cos(col_angle), jnp.sin(col_angle)])
    return (
        jnp.broadcast_to(by_row[:, :, None], (2, ROWS, LANES)),
        jnp.broadcast_to(by_col[:, None, :], (2, 8, cols)),
    )


def keep(contrast, owners, wave):
    depth, rows, cols = contrast.shape
    angs = lax.axis_size("ang")
    chips = angs // 2
    chip = lax.axis_index("ang") // 2
    by_chip = [[2 * i + c for i in range(chips)] for c in range(2)]
    first = lax.axis_index("ang") % 2 == 0
    top, bottom = contrast[:, : rows // 2], contrast[:, rows // 2 :]
    given = jnp.where(first, bottom, top)
    got = lax.ppermute(given, "ang", [(i, i ^ 1) for i in range(angs)])
    owner_chip, owner_core = owners // 2, owners % 2
    core = jnp.sum(jnp.where(owner_chip == chip, owner_core, 0))
    shared = (owner_chip[:, None] == owner_chip[None, :]).sum() > owners.shape[0]
    got, core, shared = lax.optimization_barrier((got, core, shared))
    def at(tiles, i):
        return lax.dynamic_index_in_dim(tiles, i, 0, keepdims=False)

    def one():
        kept = jnp.where(first, top, bottom)
        half = jnp.where((core == 0) == first, kept, got)
        tiles = half.reshape(rows, chips, cols // chips).transpose(1, 0, 2)
        tiles = lax.all_to_all(tiles, "ang", 0, 0, tiled=True, axis_index_groups=by_chip)
        return tuple(at(tiles, c) for c in owner_chip), wave()

    def both():
        halves = jnp.stack([jnp.where(first, top, got), jnp.where(first, got, bottom)])
        tiles = halves.reshape(2, rows, chips, cols // chips).transpose(2, 0, 1, 3)
        tiles = lax.all_to_all(tiles, "ang", 0, 0, tiled=True, axis_index_groups=by_chip)
        tiles = tiles.reshape(angs, rows, cols // chips)
        return tuple(at(tiles, o) for o in owners), wave()

    return lax.cond(shared, both, one)


def per_device(contrast, owners, tilts):
    depth, rows, cols = contrast.shape[1:]
    slabs = owners.shape[0]
    spots = lax.axis_size("xy")
    ang = lax.axis_index("ang")
    spot = lax.axis_index("xy")
    angs = lax.axis_size("ang")

    kept, wave = keep(contrast[0], owners, lambda: waves(tilts, spot * rows, rows * spots, cols))

    half = rows // 2
    slices = [(k, j, HALO[depth * k + j]) for k in range(slabs) for j in range(depth)]
    heads = [kept[k][half * j : half * j + halo] for k, j, halo in slices]
    tails = [kept[k][half * (j + 1) - halo : half * (j + 1)] for k, j, halo in slices]
    edge = jnp.where(ang % 2 == 0, jnp.concatenate(heads, axis=0), jnp.concatenate(tails, axis=0))
    up = [(spots * a + i, spots * (a + 1) + i - 1) for a in range(0, angs, 2) for i in range(1, spots)]
    edge = lax.ppermute(edge, ("ang", "xy"), up + [(j, i) for i, j in up])

    columns = [[4 * z + q for z in range(angs // 4)] for q in range(4)]
    swap_x = [(i, i ^ 2) for i in range(angs)]
    swap_core = [(i, i ^ 1) for i in range(angs)]

    def along_z(chosen, after=None):
        rims = [edge[sum(HALO[: depth * k]) : sum(HALO[: depth * (k + 1)])] for k in chosen]
        spare = jnp.zeros((-sum(r.shape[0] for r in rims) % 8, cols // (angs // 2)), jnp.float32)
        piece = jnp.concatenate([kept[k] for k in chosen] + rims + [spare], axis=0)
        if after is not None:
            piece, after = lax.optimization_barrier((piece, after))
        copies = jnp.broadcast_to(piece, (angs // 4,) + piece.shape)
        return lax.all_to_all(copies, "ang", 0, 0, tiled=True, axis_index_groups=columns)

    def from_core(mine, other):
        return lax.ppermute(jnp.stack([mine, other]), "ang", swap_core)

    early, late = (0, 1), (2,)
    mine = along_z(early)
    other = lax.ppermute(mine, "ang", swap_x)
    late_mine = along_z(late, mine)
    late_mine, other = lax.optimization_barrier((late_mine, other))
    late_other = lax.ppermute(late_mine, "ang", swap_x)
    first = mine, other, from_core(mine, other)

    place = jnp.stack([ang // 2 % 2, ang % 2, spot, jnp.int32(spots - 1)])

    def step(slab, before, pieces):
        start, end = slab == 0, slab == slabs - 1
        chosen = early if slab in early else late
        state = jax.ShapeDtypeStruct((2, ROWS, cols), jnp.float32)
        out = jax.ShapeDtypeStruct((1, rows, cols), jnp.float32)
        in_vmem = pl.BlockSpec(memory_space=pltpu.VMEM)
        return pl.pallas_call(
            functools.partial(
                through,
                slab=slab,
                place_in=(rows * chosen.index(slab), rows * len(chosen) + sum(HALO[depth * chosen[0] : depth * slab])),
                cols=cols // LANES,
                first=start,
                last=end,
            ),
            out_shape=(out, out) if end else state,
            in_specs=[pl.BlockSpec(memory_space=pltpu.SMEM)] + [in_vmem] * (len(before) + len(pieces)),
            out_specs=(pl.BlockSpec(memory_space=pl.ANY),) * 2 if end else in_vmem,
            scratch_shapes=[
                pltpu.VMEM((depth, ROWS, cols), jnp.float32),
                pltpu.VMEM(state.shape, jnp.float32),
                pltpu.VMEM(state.shape, jnp.float32),
            ]
            + ([pltpu.VMEM((2, rows, cols), jnp.float32), pltpu.SemaphoreType.DMA((2, 8))] if end else []),
            compiler_params=pltpu.CompilerParams(vmem_limit_bytes=32 * 1024 * 1024),
            cost_estimate=pl.CostEstimate(flops=20_000_000, bytes_accessed=6_000_000, transcendentals=0),
        )(place, *before, *pieces)

    field = step(1, (step(0, wave, first),), first)
    late_other, field = lax.optimization_barrier((late_other, field))
    return step(2, (field,), (late_mine, late_other, from_core(late_mine, late_other)))


def solution(mesh):
    placed = (P("ang", None, "xy", None), P(), P("ang", None))
    return jax.shard_map(
        per_device,
        mesh=mesh,
        in_specs=placed,
        out_specs=(P("ang", "xy", None), P("ang", "xy", None)),
        check_vma=False,
    )
```
